32 devices in a mesh: row: 8 (over y, x, core), col: 4 (over z).
Axes of the slice: x: 2, y: 2, z: 4, core: 2. Of those that a mesh axis runs over, the one named last changes fastest.
Arguments:
- amp_tiles: float32 [8, 4, 256, 256], P('row', 'col'), may hold values from -6 to 6
- pool_tiles: float32 [4, 256, 16, 256], P('col', 'row'), may hold values from -0.0546875 to 0.0546875
- task_amp: int32 [8, 4, 48], P('row', 'col'), may hold values from 0 to 3
- task_pool: int32 [8, 4, 48], P('row', 'col'), may hold values from 0 to 15
- task_out: int32 [8, 4, 48], P('row', 'col'), may hold values from 0 to 7
- task_live: int32 [8, 4, 48], P('row', 'col'), may hold values from 0 to 1, as said below
Outputs:
- result_tiles: float32 [4, 256, 8, 256], P('col', 'row')
The draws below stay inside these ranges and needn't reach their ends.
Inputs may be any that keep to these rules, and one draw needn't show every extreme that they name: `task_live`: on every device the live tasks come first; each device has at least a quarter of 48 live tasks, and some device has all 48 live.
All inputs are finite; a program needn't handle non-finite values.
Results may differ from the reference program's by a relative error of at most 0.0003.
Values sent between devices are 32-bit elements; how exact they have to be, the bound alone decides.
A program may use at most 128 MiB of HBM per device.

```python
import jax
import jax.numpy as jnp
from jax import lax

TS = 256
AMP_DEV = 1
POOL = 16
OUT_POOL = 8
TASK_DEV = 48
N_ROW = 8
N_COL = 4


def draw_task_live(key, part):
    key = jax.random.fold_in(key, 11)
    first_key, second_key = jax.random.split(key)
    counts = jax.random.randint(first_key, (N_ROW, N_COL), TASK_DEV // 4, TASK_DEV + 1)
    fullest = jax.random.randint(second_key, (), 0, N_ROW * N_COL)
    cells = jnp.arange(N_ROW * N_COL, dtype=jnp.int32).reshape(N_ROW, N_COL)
    counts = jnp.where(cells == fullest, TASK_DEV, counts)
    position = jnp.arange(TASK_DEV, dtype=jnp.int32)
    return (position[None, None, :] < counts[:, :, None]).astype(jnp.int32)


def set_ends(entries, stream_key, least, largest):
    extent = entries.shape
    index_at = [jax.random.randint(jax.random.fold_in(stream_key, axis), (), 0, extent[axis]) for axis in range(len(extent))]
    entries = entries.at[tuple(index_at)].set(least)
    longest = extent.index(max(extent))
    index_at[longest] = (index_at[longest] + 1) % extent[longest]
    return entries.at[tuple(index_at)].set(largest)


def levels(rng, dims, cuts, smallest, high):
    def one(axis_at, blocks):
        heights = jax.random.uniform(jax.random.fold_in(jax.random.fold_in(rng, 6), axis_at), (blocks,), jnp.float32, smallest / len(cuts), high / len(cuts))
        return jnp.repeat(jnp.exp(heights), dims[axis_at] // blocks).reshape((-1,) + (1,) * (len(dims) - axis_at - 1))

    loudness = one(*cuts[0])
    for cut in cuts[1:]:
        loudness = loudness * one(*cut)
    return loudness


def gaussian(own_key, extent, width, limit, cuts=(), kind=jnp.bfloat16):
    values = width * jax.random.normal(own_key, extent, jnp.float32)
    if cuts:
        values = values * levels(own_key, extent, cuts, -0.22, 0.18)
    return jnp.clip(values, -limit, limit).astype(kind)


def setup_inputs(seed: int = 0) -> dict:
    splits = jax.random.split(jax.random.key(seed), 7)
    amp_tiles = gaussian(splits[0], (N_ROW, N_COL * AMP_DEV, TS, TS), 1.0, 6.0, ((0, 8), (1, 4)), jnp.float32)
    pool_tiles = gaussian(splits[1], (N_COL, TS, POOL, TS), (TS * N_ROW * TASK_DEV // OUT_POOL) ** -0.5, 0.0546875, ((0, 4), (1, 8)), jnp.float32)
    task_amp = set_ends(jax.random.randint(splits[2], (N_ROW, N_COL, TASK_DEV), 0, N_COL * AMP_DEV), jax.random.fold_in(splits[2], 1), 0, (N_COL * AMP_DEV) - 1).astype(jnp.int32)
    task_pool = set_ends(jax.random.randint(splits[3], (N_ROW, N_COL, TASK_DEV), 0, POOL), jax.random.fold_in(splits[3], 1), 0, POOL - 1).astype(jnp.int32)
    task_out = set_ends(jax.random.randint(splits[4], (N_ROW, N_COL, TASK_DEV), 0, OUT_POOL), jax.random.fold_in(splits[4], 1), 0, OUT_POOL - 1).astype(jnp.int32)
    task_live = draw_task_live(jax.random.fold_in(splits[6], 71), 0)
    return {"amp_tiles": amp_tiles, "pool_tiles": pool_tiles, "task_amp": task_amp, "task_pool": task_pool, "task_out": task_out, "task_live": task_live}


def reference(amp_tiles, pool_tiles, task_amp, task_pool, task_out, task_live):
    slots = jnp.arange(OUT_POOL, dtype=jnp.int32)

    def column(index):
        pool_col = pool_tiles[index]

        def step(total, owner):
            chosen = jnp.take(amp_tiles[owner], task_amp[owner, index], axis=0)
            integral = jnp.take(pool_col, task_pool[owner, index], axis=1)
            weights = (task_out[owner, index][:, None] == slots[None, :]).astype(jnp.float32)
            weights = weights * task_live[owner, index][:, None].astype(jnp.float32)
            product = jnp.einsum("tik,ktj->tij", chosen, integral, precision=lax.Precision.HIGHEST)
            total = total + jnp.einsum("to,tij->ioj", weights, product, precision=lax.Precision.HIGHEST)
            return total, None

        start = jnp.zeros((TS, OUT_POOL, TS), jnp.float32)
        total, unused = lax.scan(step, start, jnp.arange(N_ROW, dtype=jnp.int32))
        return total

    return lax.map(column, jnp.arange(N_COL, dtype=jnp.int32))
```

```python
import functools

import jax
import jax.numpy as jnp
from jax import lax
from jax.experimental import pallas as pl
from jax.experimental.pallas import tpu as pltpu
from jax.sharding import PartitionSpec as P

OUT_POOL = 8
MESH = pl.DeviceIdType.MESH


def add_terms(piece, chosen, pool_index, weights):
    integral = jnp.take(piece[0], pool_index, axis=1)
    product = jnp.einsum("tik,ktj->tij", chosen, integral, precision=lax.Precision.HIGHEST)
    return jnp.einsum("to,tij->ioj", weights, product, precision=lax.Precision.HIGHEST)


def gathered_plan(amp_tiles, pool_tiles, task_amp, task_pool, task_out, task_live):
    slots = jnp.arange(OUT_POOL, dtype=jnp.int32)
    gathered = lax.all_gather(amp_tiles, "col", axis=1, tiled=True)
    chosen = jnp.take(gathered[0], task_amp[0, 0], axis=0)
    pool_index = task_pool[0, 0]
    live = task_live[0, 0].astype(jnp.float32)
    weights = (task_out[0, 0][:, None] == slots[None, :]).astype(jnp.float32) * live[:, None]
    whole_pool = lax.all_gather(pool_tiles, "row", axis=1, tiled=True)
    partial_value = add_terms(whole_pool, chosen, pool_index, weights)
    owned = lax.psum_scatter(partial_value, "row", scatter_dimension=0, tiled=True)
    return owned[None]


def halves(value):
    high = value.astype(jnp.bfloat16)
    low = (value - high.astype(jnp.float32)).astype(jnp.bfloat16)
    return high, low


def kernel(
    n_row, n_col, slab, pool,
    amp_ref, pool_ref, t_amp, t_pool, t_out, t_live, out_ref,
    v_all, v_hi, v_lo, a_all, m_hi, m_lo, info,
    v_send, v_recv, p_send, p_recv, i_send, i_recv, z_send, z_recv, own_sem,
):
    r = lax.axis_index("row")
    c = lax.axis_index("col")
    sib = r + 1 - 2 * (r % 2)
    x_of = r + 2 - 4 * ((r // 2) % 2)
    y_of = r + 4 - 8 * (r // 4)
    d_of = x_of + 4 - 8 * (r // 4)
    vrows = slab * pool * 2
    half = vrows // 2
    tasks = t_amp.shape[1]
    arows = slab * 2
    blk = n_row * arows
    chunk = blk // 2

    barrier = pltpu.get_barrier_semaphore()
    for d in range(1, n_row):
        pl.semaphore_signal(barrier, inc=1, device_id=(lax.rem(r + d, n_row), c), device_id_type=MESH)

    @pl.when(c > 0)
    def _():
        pl.semaphore_signal(barrier, inc=1, device_id=(r, c - 1), device_id_type=MESH)

    @pl.when(c < n_col - 1)
    def _():
        pl.semaphore_signal(barrier, inc=1, device_id=(r, c + 1), device_id_type=MESH)

    info[r] = jnp.full((8, 128), -1.0, jnp.float32)
    info[r, 0:1, 0:tasks] = t_amp[...].astype(jnp.float32)
    place = (t_pool[...] * OUT_POOL + t_out[...]).astype(jnp.float32)
    info[r, 1:2, 0:tasks] = jnp.where(t_live[...] > 0, place, -1.0)

    a_row = pl.multiple_of(c * blk + r * arows, 8)
    own_a = pltpu.make_async_copy(
        amp_ref.at[pl.ds(pl.multiple_of(r * arows, 8), arows)], a_all.at[pl.ds(a_row, arows)], own_sem.at[0])
    own_a.start()
    own_v = pltpu.make_async_copy(
        pool_ref, v_all.at[pl.ds(pl.multiple_of(r * vrows, 8), vrows)], own_sem.at[1])
    own_v.start()

    near = (c + n_col - 1) // n_col + (2 * n_col - 2 - c) // n_col
    pl.semaphore_wait(barrier, n_row - 1 + near)

    plane = []
    for d in (6, 2, 4, 3, 5, 7, 1):
        to = lax.rem(r + d, n_row)
        copy = pltpu.make_async_remote_copy(
            src_ref=amp_ref.at[pl.ds(pl.multiple_of(to * arows, 8), arows)],
            dst_ref=a_all.at[pl.ds(a_row, arows)],
            send_sem=p_send.at[d], recv_sem=p_recv.at[d],
            device_id=(to, c), device_id_type=MESH)
        copy.start()
        plane.append(copy)

    def v_copy(index, origin, part, to, own=False):
        rows = pl.ds(pl.multiple_of(origin * vrows + part * half, 8), half)
        src = pool_ref.at[pl.ds(part * half, half)] if own else v_all.at[rows]
        return pltpu.make_async_remote_copy(
            src_ref=src, dst_ref=v_all.at[rows],
            send_sem=v_send.at[index], recv_sem=v_recv.at[index],
            device_id=(to, c), device_id_type=MESH)

    v = [
        v_copy(0, r, 0, x_of, True), v_copy(1, r, 1, x_of, True),
        v_copy(2, r, 1, y_of, True), v_copy(3, r, 0, y_of, True),
        v_copy(4, r, 0, sib, True), v_copy(5, r, 1, sib, True),
        v_copy(6, x_of, 0, y_of), v_copy(7, x_of, 0, sib),
        v_copy(8, y_of, 1, x_of), v_copy(9, y_of, 1, sib),
        v_copy(10, x_of, 1, sib), v_copy(11, y_of, 0, sib),
        v_copy(12, d_of, 0, sib), v_copy(13, d_of, 1, sib),
    ]
    for index in (0, 2, 1, 3, 4, 5):
        v[index].start()

    lists = []
    for d in range(1, n_row):
        copy = pltpu.make_async_remote_copy(
            src_ref=info.at[r], dst_ref=info.at[r],
            send_sem=i_send.at[d], recv_sem=i_recv.at[d],
            device_id=(lax.rem(r + d, n_row), c), device_id_type=MESH)
        copy.start()
        lists.append(copy)

    def z_copy(way, step, part):
        tile = c - step if way == 0 else c + step
        to = c + 1 if way == 0 else c - 1
        rows = pl.ds(pl.multiple_of(tile * blk + part * chunk, 8), chunk)
        slot = ((way * (n_col - 1)) + step) * 2 + part
        return pltpu.make_async_remote_copy(
            src_ref=a_all.at[rows], dst_ref=a_all.at[rows],
            send_sem=z_send.at[slot], recv_sem=z_recv.at[slot],
            device_id=(r, to), device_id_type=MESH)

    def z_sends(way, step):
        if way == 0:
            return jnp.logical_and(c - step >= 0, c < n_col - 1)
        return jnp.logical_and(c + step < n_col, c > 0)

    def z_gets(way, step):
        return c - step - 1 >= 0 if way == 0 else c + step + 1 < n_col

    def z_start(step, part):
        for way in range(2):
            @pl.when(z_sends(way, step))
            def _():
                z_copy(way, step, part).start()

    def z_land(step, part):
        for way in range(2):
            @pl.when(z_gets(way, step))
            def _():
                z_copy(way, step, part).wait_recv()
        if step + 1 < n_col - 1:
            z_start(step + 1, part)

    def split_pool(origin):
        def one(p, carry):
            first = origin * vrows + (p // 8) * 16 + p % 8
            rows = [v_all[pl.ds(first + 8 * side, slab, stride=2 * pool), :] for side in range(2)]
            high, low = halves(jnp.concatenate(rows, axis=1))
            at = pl.ds(pl.multiple_of(origin * slab, 16), slab)
            v_hi[p, at, :] = high
            v_lo[p, at, :] = low
            return carry
        lax.fori_loop(0, pool, one, 0, unroll=4)

    own_a.wait()
    for copy in plane:
        copy.wait_recv()
    z_start(0, 0)
    z_start(0, 1)
    own_v.wait()
    split_pool(r)
    for copy in lists:
        copy.wait_recv()
    entry = lax.broadcasted_iota(jnp.int32, (pool * OUT_POOL, 128), 0).astype(jnp.float32)
    line = lax.broadcasted_iota(jnp.int32, (2 * n_col * n_row, 128), 0)
    line_row = line % n_row
    line_amp = ((line // n_row) % n_col).astype(jnp.float32)
    ends, starts = [], []
    for other in range(n_row):
        ends.append(jnp.where(entry == info[other, 1:2, :], 1.0, 0.0))
        starts.append(jnp.where(jnp.logical_and(line_row == other, line_amp == info[other, 0:1, :]), 1.0, 0.0))
    count = lax.dot_general(
        jnp.concatenate(ends, axis=1).astype(jnp.bfloat16),
        jnp.concatenate(starts, axis=1).astype(jnp.bfloat16),
        (((1,), (1,)), ((), ())), preferred_element_type=jnp.float32).astype(jnp.bfloat16)

    z_land(0, 0)
    v[0].wait_recv()
    v[6].start()
    v[7].start()
    v[2].wait_recv()
    v[8].start()
    v[9].start()
    z_land(0, 1)
    for index in (4, 5):
        v[index].wait_recv()
    split_pool(sib)
    if n_col > 2:
        z_land(1, 0)
        z_land(1, 1)
    v[1].wait_recv()
    v[10].start()
    v[3].wait_recv()
    v[11].start()
    split_pool(x_of)
    split_pool(y_of)
    for step in range(2, n_col - 1):
        z_land(step, 0)
    v[6].wait_recv()
    v[12].start()
    v[8].wait_recv()
    v[13].start()
    split_pool(d_of)
    for step in range(2, n_col - 1):
        z_land(step, 1)

    def spread(pair, carry):
        parts = []
        for k in range(2):
            i = pair * 2 + k
            first = (i // 8) * 16 + i % 8
            rows = [a_all[pl.ds(first + 8 * side, n_col * n_row, stride=arows), :] for side in range(2)]
            high, low = halves(jnp.concatenate(rows, axis=1))
            made = jnp.dot(count, jnp.concatenate([high, low], axis=0), preferred_element_type=jnp.float32)
            parts.append(made.reshape(pool, OUT_POOL, made.shape[1]))
        high, low = halves(jnp.concatenate(parts, axis=1))
        at = pl.ds(pl.multiple_of(pair * 16, 16), 16)
        m_hi[:, at, :] = high
        m_lo[:, at, :] = low
        return carry
    lax.fori_loop(0, slab // 2, spread, 0, unroll=2)

    for index in (7, 9, 10, 11, 12, 13):
        v[index].wait_recv()
    sib_x = x_of + 1 - 2 * (r % 2)
    sib_y = y_of + 1 - 2 * (r % 2)
    sib_d = d_of + 1 - 2 * (r % 2)
    split_pool(sib_x)
    split_pool(sib_y)
    split_pool(sib_d)

    total = jnp.zeros(out_ref.shape, jnp.float32)
    for p in range(pool):
        total = total + jnp.dot(m_hi[p], v_hi[p], preferred_element_type=jnp.float32)
        total = total + jnp.dot(m_hi[p], v_lo[p], preferred_element_type=jnp.float32)
        total = total + jnp.dot(m_lo[p], v_hi[p], preferred_element_type=jnp.float32)
    out_ref[...] = total

    for copy in plane + lists + v:
        copy.wait_send()
    for step in range(n_col - 1):
        for way in range(2):
            @pl.when(z_sends(way, step))
            def _():
                for part in range(2):
                    z_copy(way, step, part).wait_send()


def by_side(rows):
    count, width = rows.shape
    blocks = rows.reshape(count // 8, 8, 2, width // 2).transpose(0, 2, 1, 3)
    return blocks.reshape(2 * count, width // 2)


def slab_plan(n_row, n_col, amp_tiles, pool_tiles, task_amp, task_pool, task_out, task_live):
    ts = amp_tiles.shape[-1]
    slab, pool = pool_tiles.shape[1], pool_tiles.shape[2]
    vmem = pl.BlockSpec(memory_space=pltpu.VMEM)
    hbm = pl.BlockSpec(memory_space=pl.ANY)
    dma = pltpu.SemaphoreType.DMA
    out = pl.pallas_call(
        functools.partial(kernel, n_row, n_col, slab, pool),
        out_shape=jax.ShapeDtypeStruct((slab * OUT_POOL, ts), jnp.float32),
        in_specs=[hbm, hbm, vmem, vmem, vmem, vmem],
        out_specs=vmem,
        scratch_shapes=[
            pltpu.VMEM((2 * ts * pool, ts // 2), jnp.float32),
            pltpu.VMEM((pool, ts, ts), jnp.bfloat16),
            pltpu.VMEM((pool, ts, ts), jnp.bfloat16),
            pltpu.VMEM((2 * n_col * n_row * slab, ts // 2), jnp.float32),
            pltpu.VMEM((pool, slab * OUT_POOL, ts), jnp.bfloat16),
            pltpu.VMEM((pool, slab * OUT_POOL, ts), jnp.bfloat16),
            pltpu.VMEM((n_row, 8, 128), jnp.float32),
            dma((14,)), dma((14,)),
            dma((n_row,)), dma((n_row,)),
            dma((n_row,)), dma((n_row,)),
            dma((4 * (n_col - 1),)), dma((4 * (n_col - 1),)),
            dma((2,)),
        ],
        compiler_params=pltpu.CompilerParams(
            collective_id=0, has_side_effects=True, vmem_limit_bytes=40 * 2**20),
    )(
        by_side(amp_tiles.reshape(ts, ts)), by_side(pool_tiles.reshape(slab * pool, ts)),
        task_amp[0], task_pool[0], task_out[0], task_live[0],
    )
    return out.reshape(1, slab, OUT_POOL, ts)


def solution(mesh):
    n_row, n_col = mesh.shape["row"], mesh.shape["col"]

    def per_device(*arrays):
        amp_tiles, pool_tiles, task_amp = arrays[0], arrays[1], arrays[2]
        fits = (
            n_row == 8 and n_col > 1 and amp_tiles.shape[3] == 256 and amp_tiles.shape[1] == 1
            and pool_tiles.shape[1] % 16 == 0 and pool_tiles.shape[2] * OUT_POOL == 128
            and task_amp.shape[-1] <= 128 and 2 * n_col * n_row <= 256
        )
        if fits:
            return slab_plan(n_row, n_col, *arrays)
        return gathered_plan(*arrays)

    in_specs = (
        P("row", "col", None, None),
        P("col", "row", None, None),
        P("row", "col", None),
        P("row", "col", None),
        P("row", "col", None),
        P("row", "col", None),
    )
    out_specs = P("col", "row", None, None)
    return jax.shard_map(
        per_device, mesh=mesh, in_specs=in_specs, out_specs=out_specs, check_vma=False
    )
```

```python
import functools

import jax
import jax.numpy as jnp
from jax import lax
from jax.experimental import pallas as pl
from jax.experimental.pallas import tpu as pltpu
from jax.sharding import PartitionSpec as P

OUT_POOL = 8
MESH = pl.DeviceIdType.MESH


def add_terms(piece, chosen, pool_index, weights):
    integral = jnp.take(piece[0], pool_index, axis=1)
    product = jnp.einsum("tik,ktj->tij", chosen, integral, precision=lax.Precision.HIGHEST)
    return jnp.einsum("to,tij->ioj", weights, product, precision=lax.Precision.HIGHEST)


def gathered_plan(amp_tiles, pool_tiles, task_amp, task_pool, task_out, task_live):
    slots = jnp.arange(OUT_POOL, dtype=jnp.int32)
    gathered = lax.all_gather(amp_tiles, "col", axis=1, tiled=True)
    chosen = jnp.take(gathered[0], task_amp[0, 0], axis=0)
    pool_index = task_pool[0, 0]
    live = task_live[0, 0].astype(jnp.float32)
    weights = (task_out[0, 0][:, None] == slots[None, :]).astype(jnp.float32) * live[:, None]
    whole_pool = lax.all_gather(pool_tiles, "row", axis=1, tiled=True)
    partial_value = add_terms(whole_pool, chosen, pool_index, weights)
    owned = lax.psum_scatter(partial_value, "row", scatter_dimension=0, tiled=True)
    return owned[None]


def halves(value):
    high = value.astype(jnp.bfloat16)
    low = (value - high.astype(jnp.float32)).astype(jnp.bfloat16)
    return high, low


def kernel(
    n_row, n_col, slab, pool,
    amp_ref, pool_ref, t_amp, t_pool, t_out, t_live, out_ref,
    v_all, v_hi, v_lo, a_all, m_hi, m_lo, info,
    v_send, v_recv, p_send, p_recv, i_send, i_recv, z_send, z_recv, own_sem,
):
    r = lax.axis_index("row")
    c = lax.axis_index("col")
    sib = r + 1 - 2 * (r % 2)
    x_of = r + 2 - 4 * ((r // 2) % 2)
    y_of = r + 4 - 8 * (r // 4)
    d_of = x_of + 4 - 8 * (r // 4)
    vrows = slab * pool * 2
    piece = vrows // 4
    tasks = t_amp.shape[1]
    arows = slab * 2
    blk = n_row * arows

    barrier = pltpu.get_barrier_semaphore()
    for d in range(1, n_row):
        pl.semaphore_signal(barrier, inc=1, device_id=(lax.rem(r + d, n_row), c), device_id_type=MESH)

    @pl.when(c > 0)
    def _():
        pl.semaphore_signal(barrier, inc=1, device_id=(r, c - 1), device_id_type=MESH)

    @pl.when(c < n_col - 1)
    def _():
        pl.semaphore_signal(barrier, inc=1, device_id=(r, c + 1), device_id_type=MESH)

    info[r] = jnp.full((8, 128), -1.0, jnp.float32)
    info[r, 0:1, 0:tasks] = t_amp[...].astype(jnp.float32)
    place = (t_pool[...] * OUT_POOL + t_out[...]).astype(jnp.float32)
    info[r, 1:2, 0:tasks] = jnp.where(t_live[...] > 0, place, -1.0)

    a_row = pl.multiple_of(c * blk + r * arows, 8)
    own_a = pltpu.make_async_copy(
        amp_ref.at[pl.ds(pl.multiple_of(r * arows, 8), arows)], a_all.at[pl.ds(a_row, arows)], own_sem.at[0])
    own_a.start()
    own_v = pltpu.make_async_copy(
        pool_ref, v_all.at[pl.ds(pl.multiple_of(r * vrows, 8), vrows)], own_sem.at[1])
    own_v.start()

    near = (c + n_col - 1) // n_col + (2 * n_col - 2 - c) // n_col
    pl.semaphore_wait(barrier, n_row - 1 + near)

    sib_x = x_of + 1 - 2 * (r % 2)
    sib_y = y_of + 1 - 2 * (r % 2)
    sib_d = d_of + 1 - 2 * (r % 2)
    peers = (sib, sib_x, x_of, sib_y, y_of, sib_d, d_of)

    plane = []
    for k, to in enumerate(peers):
        copy = pltpu.make_async_remote_copy(
            src_ref=amp_ref.at[pl.ds(pl.multiple_of(to * arows, 8), arows)],
            dst_ref=a_all.at[pl.ds(a_row, arows)],
            send_sem=p_send.at[k], recv_sem=p_recv.at[k],
            device_id=(to, c), device_id_type=MESH)
        copy.start()
        plane.append(copy)

    def v_copy(index, origin, part, to, own=False):
        rows = pl.ds(pl.multiple_of(origin * vrows + part * piece, 8), piece)
        src = pool_ref.at[pl.ds(part * piece, piece)] if own else v_all.at[rows]
        return pltpu.make_async_remote_copy(
            src_ref=src, dst_ref=v_all.at[rows],
            send_sem=v_send.at[index], recv_sem=v_recv.at[index],
            device_id=(to, c), device_id_type=MESH)

    to_x = [v_copy(q, r, q, x_of, True) for q in range(4)]
    to_y = [v_copy(4 + q, r, q, y_of, True) for q in range(4)]
    to_s = [v_copy(8 + q, r, q, sib, True) for q in range(4)]
    far = [v_copy(12 + q, x_of, q, y_of) if q < 2 else v_copy(12 + q, y_of, q, x_of) for q in range(4)]
    x_s = [v_copy(16 + q, x_of, q, sib) for q in range(4)]
    y_s = [v_copy(20 + q, y_of, q, sib) for q in range(4)]
    d_s = [v_copy(24 + q, d_of, q, sib) for q in range(4)]
    for q in range(4):
        to_x[q].start()
        to_y[3 - q].start()
    for q in range(4):
        to_s[q].start()

    lists = []
    for k, to in enumerate(peers):
        copy = pltpu.make_async_remote_copy(
            src_ref=info.at[r], dst_ref=info.at[r],
            send_sem=i_send.at[k], recv_sem=i_recv.at[k],
            device_id=(to, c), device_id_type=MESH)
        copy.start()
        lists.append(copy)

    bases = [one - one % 2 for one in (r, x_of, y_of, d_of)]

    def z_copy(way, step, part):
        tile = c - step if way == 0 else c + step
        to = c + 1 if way == 0 else c - 1
        rows = pl.ds(pl.multiple_of(tile * blk + bases[part] * arows, 8), 2 * arows)
        slot = ((way * (n_col - 1)) + step) * 4 + part
        return pltpu.make_async_remote_copy(
            src_ref=a_all.at[rows], dst_ref=a_all.at[rows],
            send_sem=z_send.at[slot], recv_sem=z_recv.at[slot],
            device_id=(r, to), device_id_type=MESH)

    def z_sends(way, step):
        if way == 0:
            return jnp.logical_and(c - step >= 0, c < n_col - 1)
        return jnp.logical_and(c + step < n_col, c > 0)

    def z_gets(way, step):
        return c - step - 1 >= 0 if way == 0 else c + step + 1 < n_col

    def z_start(step, part):
        for way in range(2):
            @pl.when(z_sends(way, step))
            def _():
                z_copy(way, step, part).start()

    def z_land(step, part):
        for way in range(2):
            @pl.when(z_gets(way, step))
            def _():
                z_copy(way, step, part).wait_recv()
        if step + 1 < n_col - 1:
            z_start(step + 1, part)

    def near_land(q):
        to_x[q].wait_recv()
        if q < 2:
            far[q].start()
        x_s[q].start()
        to_y[3 - q].wait_recv()
        if q < 2:
            far[3 - q].start()
        y_s[3 - q].start()

    def far_land(q):
        for one in (q, 3 - q):
            far[one].wait_recv()
            d_s[one].start()

    def split_pool(origin):
        def one(p, carry):
            first = origin * vrows + (p // 8) * 16 + p % 8
            rows = [v_all[pl.ds(first + 8 * side, slab, stride=2 * pool), :] for side in range(2)]
            high, low = halves(jnp.concatenate(rows, axis=1))
            at = pl.ds(pl.multiple_of(origin * slab, 16), slab)
            v_hi[p, at, :] = high
            v_lo[p, at, :] = low
            return carry
        lax.fori_loop(0, pool, one, 0, unroll=4)

    own_a.wait()
    plane[0].wait_recv()
    z_start(0, 0)
    for part in range(1, 4):
        plane[2 * part - 1].wait_recv()
        plane[2 * part].wait_recv()
        z_start(0, part)
    own_v.wait()
    split_pool(r)

    z_events = [(step, part) for step in range(n_col - 1) for part in range(4)]
    v_events = [(near_land, 0), (near_land, 1), (near_land, 2), (near_land, 3), (far_land, 0), (far_land, 1)]
    order = z_events[:2]
    rest = z_events[2:]
    for at, event in enumerate(v_events):
        share = len(rest) * (at + 1) // (len(v_events) + 1)
        done = len(rest) * at // (len(v_events) + 1)
        order = order + rest[done:share] + [event]
    order = order + rest[len(rest) * len(v_events) // (len(v_events) + 1):]
    for first, second in order:
        if callable(first):
            first(second)
            if (first, second) == v_events[1]:
                for copy in to_s:
                    copy.wait_recv()
                split_pool(sib)
            if (first, second) == v_events[3]:
                split_pool(x_of)
                split_pool(y_of)
            if (first, second) == v_events[4]:
                for copy in x_s + y_s:
                    copy.wait_recv()
                split_pool(sib_x)
                split_pool(sib_y)
        else:
            z_land(first, second)
    split_pool(d_of)

    for copy in lists:
        copy.wait_recv()
    entry = lax.broadcasted_iota(jnp.int32, (pool * OUT_POOL, 128), 0).astype(jnp.float32)
    line = lax.broadcasted_iota(jnp.int32, (2 * n_col * n_row, 128), 0)
    line_row = line % n_row
    line_amp = ((line // n_row) % n_col).astype(jnp.float32)
    ends, starts = [], []
    for other in range(n_row):
        ends.append(jnp.where(entry == info[other, 1:2, :], 1.0, 0.0))
        starts.append(jnp.where(jnp.logical_and(line_row == other, line_amp == info[other, 0:1, :]), 1.0, 0.0))
    count = lax.dot_general(
        jnp.concatenate(ends, axis=1).astype(jnp.bfloat16),
        jnp.concatenate(starts, axis=1).astype(jnp.bfloat16),
        (((1,), (1,)), ((), ())), preferred_element_type=jnp.float32).astype(jnp.bfloat16)

    def spread(pair, carry):
        parts = []
        for k in range(2):
            i = pair * 2 + k
            first = (i // 8) * 16 + i % 8
            rows = [a_all[pl.ds(first + 8 * side, n_col * n_row, stride=arows), :] for side in range(2)]
            high, low = halves(jnp.concatenate(rows, axis=1))
            made = jnp.dot(count, jnp.concatenate([high, low], axis=0), preferred_element_type=jnp.float32)
            parts.append(made.reshape(pool, OUT_POOL, made.shape[1]))
        high, low = halves(jnp.concatenate(parts, axis=1))
        at = pl.ds(pl.multiple_of(pair * 16, 16), 16)
        m_hi[:, at, :] = high
        m_lo[:, at, :] = low
        return carry
    lax.fori_loop(0, slab // 2, spread, 0, unroll=4)

    for copy in d_s:
        copy.wait_recv()
    split_pool(sib_d)

    total = jnp.zeros(out_ref.shape, jnp.float32)
    for p in range(pool):
        total = total + jnp.dot(m_hi[p], v_hi[p], preferred_element_type=jnp.float32)
        total = total + jnp.dot(m_hi[p], v_lo[p], preferred_element_type=jnp.float32)
        total = total + jnp.dot(m_lo[p], v_hi[p], preferred_element_type=jnp.float32)
    out_ref[...] = total

    for copy in plane + lists + to_x + to_y + to_s + far + x_s + y_s + d_s:
        copy.wait_send()
    for step in range(n_col - 1):
        for way in range(2):
            @pl.when(z_sends(way, step))
            def _():
                for part in range(4):
                    z_copy(way, step, part).wait_send()


def by_side(rows):
    count, width = rows.shape
    blocks = rows.reshape(count // 8, 8, 2, width // 2).transpose(0, 2, 1, 3)
    return blocks.reshape(2 * count, width // 2)


def slab_plan(n_row, n_col, amp_tiles, pool_tiles, task_amp, task_pool, task_out, task_live):
    ts = amp_tiles.shape[-1]
    slab, pool = pool_tiles.shape[1], pool_tiles.shape[2]
    vmem = pl.BlockSpec(memory_space=pltpu.VMEM)
    hbm = pl.BlockSpec(memory_space=pl.ANY)
    dma = pltpu.SemaphoreType.DMA
    out = pl.pallas_call(
        functools.partial(kernel, n_row, n_col, slab, pool),
        out_shape=jax.ShapeDtypeStruct((slab * OUT_POOL, ts), jnp.float32),
        in_specs=[hbm, hbm, vmem, vmem, vmem, vmem],
        out_specs=vmem,
        scratch_shapes=[
            pltpu.VMEM((2 * ts * pool, ts // 2), jnp.float32),
            pltpu.VMEM((pool, ts, ts), jnp.bfloat16),
            pltpu.VMEM((pool, ts, ts), jnp.bfloat16),
            pltpu.VMEM((2 * n_col * n_row * slab, ts // 2), jnp.float32),
            pltpu.VMEM((pool, slab * OUT_POOL, ts), jnp.bfloat16),
            pltpu.VMEM((pool, slab * OUT_POOL, ts), jnp.bfloat16),
            pltpu.VMEM((n_row, 8, 128), jnp.float32),
            dma((28,)), dma((28,)),
            dma((n_row,)), dma((n_row,)),
            dma((n_row,)), dma((n_row,)),
            dma((8 * (n_col - 1),)), dma((8 * (n_col - 1),)),
            dma((2,)),
        ],
        compiler_params=pltpu.CompilerParams(
            collective_id=0, has_side_effects=True, vmem_limit_bytes=60 * 2**20),
    )(
        by_side(amp_tiles.reshape(ts, ts)), by_side(pool_tiles.reshape(slab * pool, ts)),
        task_amp[0], task_pool[0], task_out[0], task_live[0],
    )
    return out.reshape(1, slab, OUT_POOL, ts)


def solution(mesh):
    n_row, n_col = mesh.shape["row"], mesh.shape["col"]

    def per_device(*arrays):
        amp_tiles, pool_tiles, task_amp = arrays[0], arrays[1], arrays[2]
        fits = (
            n_row == 8 and n_col > 1 and amp_tiles.shape[3] == 256 and amp_tiles.shape[1] == 1
            and pool_tiles.shape[1] % 16 == 0 and pool_tiles.shape[2] * OUT_POOL == 128
            and task_amp.shape[-1] <= 128 and 2 * n_col * n_row <= 256
        )
        if fits:
            return slab_plan(n_row, n_col, *arrays)
        return gathered_plan(*arrays)

    in_specs = (
        P("row", "col", None, None),
        P("col", "row", None, None),
        P("row", "col", None),
        P("row", "col", None),
        P("row", "col", None),
        P("row", "col", None),
    )
    out_specs = P("col", "row", None, None)
    return jax.shard_map(
        per_device, mesh=mesh, in_specs=in_specs, out_specs=out_specs, check_vma=False
    )
```

```python
import functools

import jax
import jax.numpy as jnp
from jax import lax
from jax.experimental import pallas as pl
from jax.experimental.pallas import tpu as pltpu
from jax.sharding import PartitionSpec as P

OUT_POOL = 8
MESH = pl.DeviceIdType.MESH


def add_terms(piece, chosen, pool_index, weights):
    integral = jnp.take(piece[0], pool_index, axis=1)
    product = jnp.einsum("tik,ktj->tij", chosen, integral, precision=lax.Precision.HIGHEST)
    return jnp.einsum("to,tij->ioj", weights, product, precision=lax.Precision.HIGHEST)


def gathered_plan(amp_tiles, pool_tiles, task_amp, task_pool, task_out, task_live):
    slots = jnp.arange(OUT_POOL, dtype=jnp.int32)
    gathered = lax.all_gather(amp_tiles, "col", axis=1, tiled=True)
    chosen = jnp.take(gathered[0], task_amp[0, 0], axis=0)
    pool_index = task_pool[0, 0]
    live = task_live[0, 0].astype(jnp.float32)
    weights = (task_out[0, 0][:, None] == slots[None, :]).astype(jnp.float32) * live[:, None]
    whole_pool = lax.all_gather(pool_tiles, "row", axis=1, tiled=True)
    partial_value = add_terms(whole_pool, chosen, pool_index, weights)
    owned = lax.psum_scatter(partial_value, "row", scatter_dimension=0, tiled=True)
    return owned[None]


def halves(value):
    high = value.astype(jnp.bfloat16)
    low = (value - high.astype(jnp.float32)).astype(jnp.bfloat16)
    return high, low


def kernel(
    n_row, n_col, slab, pool,
    amp_ref, pool_ref, t_amp, t_pool, t_out, t_live, out_ref,
    v_all, v_hi, v_lo, a_all, m_hi, m_lo, info,
    v_send, v_recv, p_send, p_recv, i_send, i_recv, z_send, z_recv, own_sem,
):
    r = lax.axis_index("row")
    c = lax.axis_index("col")
    sib = r + 1 - 2 * (r % 2)
    x_of = r + 2 - 4 * ((r // 2) % 2)
    y_of = r + 4 - 8 * (r // 4)
    d_of = x_of + 4 - 8 * (r // 4)
    vrows = slab * pool * 2
    piece = vrows // 4
    tasks = t_amp.shape[1]
    arows = slab * 2
    blk = n_row * arows

    barrier = pltpu.get_barrier_semaphore()
    for d in range(1, n_row):
        pl.semaphore_signal(barrier, inc=1, device_id=(lax.rem(r + d, n_row), c), device_id_type=MESH)

    @pl.when(c > 0)
    def _():
        pl.semaphore_signal(barrier, inc=1, device_id=(r, c - 1), device_id_type=MESH)

    @pl.when(c < n_col - 1)
    def _():
        pl.semaphore_signal(barrier, inc=1, device_id=(r, c + 1), device_id_type=MESH)

    info[r] = jnp.full((8, 128), -1.0, jnp.float32)
    info[r, 0:1, 0:tasks] = t_amp[...].astype(jnp.float32)
    place = (t_pool[...] * OUT_POOL + t_out[...]).astype(jnp.float32)
    info[r, 1:2, 0:tasks] = jnp.where(t_live[...] > 0, place, -1.0)

    a_row = pl.multiple_of(c * blk + r * arows, 8)
    own_a = pltpu.make_async_copy(
        amp_ref.at[pl.ds(pl.multiple_of(r * arows, 8), arows)], a_all.at[pl.ds(a_row, arows)], own_sem.at[0])
    own_a.start()
    own_v = pltpu.make_async_copy(
        pool_ref, v_all.at[pl.ds(pl.multiple_of(r * vrows, 8), vrows)], own_sem.at[1])
    own_v.start()

    near = (c + n_col - 1) // n_col + (2 * n_col - 2 - c) // n_col
    pl.semaphore_wait(barrier, n_row - 1 + near)

    sib_x = x_of + 1 - 2 * (r % 2)
    sib_y = y_of + 1 - 2 * (r % 2)
    sib_d = d_of + 1 - 2 * (r % 2)
    peers = (sib, sib_x, x_of, sib_y, y_of, sib_d, d_of)

    plane = []
    for k, to in enumerate(peers):
        copy = pltpu.make_async_remote_copy(
            src_ref=amp_ref.at[pl.ds(pl.multiple_of(to * arows, 8), arows)],
            dst_ref=a_all.at[pl.ds(a_row, arows)],
            send_sem=p_send.at[k], recv_sem=p_recv.at[k],
            device_id=(to, c), device_id_type=MESH)
        copy.start()
        plane.append(copy)

    lists = []
    for k, to in enumerate(peers):
        copy = pltpu.make_async_remote_copy(
            src_ref=info.at[r], dst_ref=info.at[r],
            send_sem=i_send.at[k], recv_sem=i_recv.at[k],
            device_id=(to, c), device_id_type=MESH)
        copy.start()
        lists.append(copy)

    def v_copy(index, origin, part, to, own=False):
        rows = pl.ds(pl.multiple_of(origin * vrows + part * piece, 8), piece)
        src = pool_ref.at[pl.ds(part * piece, piece)] if own else v_all.at[rows]
        return pltpu.make_async_remote_copy(
            src_ref=src, dst_ref=v_all.at[rows],
            send_sem=v_send.at[index], recv_sem=v_recv.at[index],
            device_id=(to, c), device_id_type=MESH)

    to_x = [v_copy(q, r, q, x_of, True) for q in range(4)]
    to_y = [v_copy(4 + q, r, q, y_of, True) for q in range(4)]
    to_s = [v_copy(8 + q, r, q, sib, True) for q in range(4)]
    far = [v_copy(12 + q, x_of, q, y_of) if q < 2 else v_copy(12 + q, y_of, q, x_of) for q in range(4)]
    x_s = [v_copy(16 + q, x_of, q, sib) for q in range(4)]
    y_s = [v_copy(20 + q, y_of, q, sib) for q in range(4)]
    d_s = [v_copy(24 + q, d_of, q, sib) for q in range(4)]
    for q in range(4):
        to_x[q].start()
        to_y[3 - q].start()
    for q in range(4):
        to_s[q].start()

    bases = [one - one % 2 for one in (r, x_of, y_of, d_of)]

    def z_copy(way, step, part):
        tile = c - step if way == 0 else c + step
        to = c + 1 if way == 0 else c - 1
        rows = pl.ds(pl.multiple_of(tile * blk + bases[part] * arows, 8), 2 * arows)
        slot = ((way * (n_col - 1)) + step) * 4 + part
        return pltpu.make_async_remote_copy(
            src_ref=a_all.at[rows], dst_ref=a_all.at[rows],
            send_sem=z_send.at[slot], recv_sem=z_recv.at[slot],
            device_id=(r, to), device_id_type=MESH)

    def z_sends(way, step):
        if way == 0:
            return jnp.logical_and(c - step >= 0, c < n_col - 1)
        return jnp.logical_and(c + step < n_col, c > 0)

    def z_gets(way, step):
        return c - step - 1 >= 0 if way == 0 else c + step + 1 < n_col

    def z_start(step, part):
        for way in range(2):
            @pl.when(z_sends(way, step))
            def _():
                z_copy(way, step, part).start()

    def z_land(step, part):
        for way in range(2):
            @pl.when(z_gets(way, step))
            def _():
                z_copy(way, step, part).wait_recv()
        if step + 1 < n_col - 1:
            z_start(step + 1, part)

    def near_land(q):
        to_x[q].wait_recv()
        if q < 2:
            far[q].start()
        x_s[q].start()
        to_y[3 - q].wait_recv()
        if q < 2:
            far[3 - q].start()
        y_s[3 - q].start()

    def far_land(q):
        for one in (q, 3 - q):
            far[one].wait_recv()
            d_s[one].start()

    def split_pool(origin):
        def one(p, carry):
            first = origin * vrows + (p // 8) * 16 + p % 8
            rows = [v_all[pl.ds(first + 8 * side, slab, stride=2 * pool), :] for side in range(2)]
            high, low = halves(jnp.concatenate(rows, axis=1))
            at = pl.ds(pl.multiple_of(origin * slab, 16), slab)
            v_hi[p, at, :] = high
            v_lo[p, at, :] = low
            return carry
        lax.fori_loop(0, pool, one, 0, unroll=4)

    def count_tasks():
        for copy in lists:
            copy.wait_recv()
        entry = lax.broadcasted_iota(jnp.int32, (pool * OUT_POOL, 128), 0).astype(jnp.float32)
        line = lax.broadcasted_iota(jnp.int32, (2 * n_col * n_row, 128), 0)
        line_row = line % n_row
        line_amp = ((line // n_row) % n_col).astype(jnp.float32)
        ends, starts = [], []
        for other in range(n_row):
            ends.append(jnp.where(entry == info[other, 1:2, :], 1.0, 0.0))
            starts.append(jnp.where(jnp.logical_and(line_row == other, line_amp == info[other, 0:1, :]), 1.0, 0.0))
        return lax.dot_general(
            jnp.concatenate(ends, axis=1).astype(jnp.bfloat16),
            jnp.concatenate(starts, axis=1).astype(jnp.bfloat16),
            (((1,), (1,)), ((), ())), preferred_element_type=jnp.float32).astype(jnp.bfloat16)

    own_a.wait()
    plane[0].wait_recv()
    z_start(0, 0)
    for part in range(1, 4):
        plane[2 * part - 1].wait_recv()
        plane[2 * part].wait_recv()
        z_start(0, part)
    own_v.wait()
    split_pool(r)

    z_events = [(step, part) for step in range(n_col - 1) for part in range(4)]
    v_events = [(near_land, 0), (near_land, 1), (near_land, 2), (near_land, 3), (far_land, 0), (far_land, 1)]
    order = z_events[:2]
    rest = z_events[2:]
    for at, event in enumerate(v_events):
        share = len(rest) * (at + 1) // (len(v_events) + 1)
        done = len(rest) * at // (len(v_events) + 1)
        order = order + rest[done:share] + [event]
    order = order + rest[len(rest) * len(v_events) // (len(v_events) + 1):]
    for first, second in order:
        if callable(first):
            first(second)
            if (first, second) == v_events[1]:
                for copy in to_s:
                    copy.wait_recv()
                split_pool(sib)
            if (first, second) == v_events[2]:
                count = count_tasks()
            if (first, second) == v_events[3]:
                split_pool(x_of)
                split_pool(y_of)
            if (first, second) == v_events[4]:
                for copy in x_s + y_s:
                    copy.wait_recv()
                split_pool(sib_x)
                split_pool(sib_y)
        else:
            z_land(first, second)
    split_pool(d_of)

    def spread(pair, carry):
        parts = []
        for k in range(2):
            i = pair * 2 + k
            first = (i // 8) * 16 + i % 8
            rows = [a_all[pl.ds(first + 8 * side, n_col * n_row, stride=arows), :] for side in range(2)]
            high, low = halves(jnp.concatenate(rows, axis=1))
            made = jnp.dot(count, jnp.concatenate([high, low], axis=0), preferred_element_type=jnp.float32)
            parts.append(made.reshape(pool, OUT_POOL, made.shape[1]))
        high, low = halves(jnp.concatenate(parts, axis=1))
        at = pl.ds(pl.multiple_of(pair * 16, 16), 16)
        m_hi[:, at, :] = high
        m_lo[:, at, :] = low
        return carry
    lax.fori_loop(0, slab // 2, spread, 0, unroll=8)

    for copy in d_s:
        copy.wait_recv()
    split_pool(sib_d)

    total = jnp.zeros(out_ref.shape, jnp.float32)
    for p in range(pool):
        total = total + jnp.dot(m_hi[p], v_hi[p], preferred_element_type=jnp.float32)
        total = total + jnp.dot(m_hi[p], v_lo[p], preferred_element_type=jnp.float32)
        total = total + jnp.dot(m_lo[p], v_hi[p], preferred_element_type=jnp.float32)
    out_ref[...] = total

    for copy in plane + lists + to_x + to_y + to_s + far + x_s + y_s + d_s:
        copy.wait_send()
    for step in range(n_col - 1):
        for way in range(2):
            @pl.when(z_sends(way, step))
            def _():
                for part in range(4):
                    z_copy(way, step, part).wait_send()


def by_side(rows):
    count, width = rows.shape
    blocks = rows.reshape(count // 8, 8, 2, width // 2).transpose(0, 2, 1, 3)
    return blocks.reshape(2 * count, width // 2)


def slab_plan(n_row, n_col, amp_tiles, pool_tiles, task_amp, task_pool, task_out, task_live):
    ts = amp_tiles.shape[-1]
    slab, pool = pool_tiles.shape[1], pool_tiles.shape[2]
    vmem = pl.BlockSpec(memory_space=pltpu.VMEM)
    hbm = pl.BlockSpec(memory_space=pl.ANY)
    dma = pltpu.SemaphoreType.DMA
    out = pl.pallas_call(
        functools.partial(kernel, n_row, n_col, slab, pool),
        out_shape=jax.ShapeDtypeStruct((slab * OUT_POOL, ts), jnp.float32),
        in_specs=[hbm, hbm, vmem, vmem, vmem, vmem],
        out_specs=vmem,
        scratch_shapes=[
            pltpu.VMEM((2 * ts * pool, ts // 2), jnp.float32),
            pltpu.VMEM((pool, ts, ts), jnp.bfloat16),
            pltpu.VMEM((pool, ts, ts), jnp.bfloat16),
            pltpu.VMEM((2 * n_col * n_row * slab, ts // 2), jnp.float32),
            pltpu.VMEM((pool, slab * OUT_POOL, ts), jnp.bfloat16),
            pltpu.VMEM((pool, slab * OUT_POOL, ts), jnp.bfloat16),
            pltpu.VMEM((n_row, 8, 128), jnp.float32),
            dma((28,)), dma((28,)),
            dma((n_row,)), dma((n_row,)),
            dma((n_row,)), dma((n_row,)),
            dma((8 * (n_col - 1),)), dma((8 * (n_col - 1),)),
            dma((2,)),
        ],
        compiler_params=pltpu.CompilerParams(
            collective_id=0, has_side_effects=True, vmem_limit_bytes=60 * 2**20),
    )(
        by_side(amp_tiles.reshape(ts, ts)), by_side(pool_tiles.reshape(slab * pool, ts)),
        task_amp[0], task_pool[0], task_out[0], task_live[0],
    )
    return out.reshape(1, slab, OUT_POOL, ts)


def solution(mesh):
    n_row, n_col = mesh.shape["row"], mesh.shape["col"]

    def per_device(*arrays):
        amp_tiles, pool_tiles, task_amp = arrays[0], arrays[1], arrays[2]
        fits = (
            n_row == 8 and n_col > 1 and amp_tiles.shape[3] == 256 and amp_tiles.shape[1] == 1
            and pool_tiles.shape[1] % 16 == 0 and pool_tiles.shape[2] * OUT_POOL == 128
            and task_amp.shape[-1] <= 128 and 2 * n_col * n_row <= 256
        )
        if fits:
            return slab_plan(n_row, n_col, *arrays)
        return gathered_plan(*arrays)

    in_specs = (
        P("row", "col", None, None),
        P("col", "row", None, None),
        P("row", "col", None),
        P("row", "col", None),
        P("row", "col", None),
        P("row", "col", None),
    )
    out_specs = P("col", "row", None, None)
    return jax.shard_map(
        per_device, mesh=mesh, in_specs=in_specs, out_specs=out_specs, check_vma=False
    )
```
